32 devices in a mesh: rep: 4 (over x, core), shard: 8 (over z, y).
Axes of the slice: x: 2, y: 2, z: 4, core: 2. Of those that a mesh axis runs over, the one named last changes fastest.
Arguments:
- tokens: bfloat16 [16384, 1024], P(('rep', 'shard')), may hold values from -6 to 6
- cotangent: bfloat16 [16384, 1024], P(('rep', 'shard')), may hold values from -6 to 6
- attn_gain: bfloat16 [1024], P('shard'), may hold values from 0.5 to 1.5
- query_gain: bfloat16 [128], P('shard'), may hold values from 0.25 to 1.75
- key_gain: bfloat16 [128], P('shard'), may hold values from 0.25 to 1.75
- query_proj: bfloat16 [1024, 2048], P('shard'), may hold values from -0.1875 to 0.1875
- key_proj: bfloat16 [1024, 1024], P('shard'), may hold values from -0.1875 to 0.1875
- value_proj: bfloat16 [1024, 1024], P('shard'), may hold values from -0.1875 to 0.1875
- out_proj: bfloat16 [2048, 1024], P('shard'), may hold values from -0.75 to 0.75
- mlp_gain: bfloat16 [1024], P('shard'), may hold values from 0.5 to 1.5
- gate_proj: bfloat16 [1024, 3072], P('shard'), may hold values from -0.1875 to 0.1875
- up_proj: bfloat16 [1024, 3072], P('shard'), may hold values from -0.1875 to 0.1875
- down_proj: bfloat16 [3072, 1024], P('shard'), may hold values from -0.109375 to 0.109375
Outputs:
- layer_out: bfloat16 [16384, 1024], P(('rep', 'shard'))
- tokens_grad: float32 [16384, 1024], P(('rep', 'shard'))
- attn_gain_grad: float32 [1024], P('shard')
- query_gain_grad: float32 [128], P('shard')
- key_gain_grad: float32 [128], P('shard')
- query_proj_grad: float32 [1024, 2048], P('shard')
- key_proj_grad: float32 [1024, 1024], P('shard')
- value_proj_grad: float32 [1024, 1024], P('shard')
- out_proj_grad: float32 [2048, 1024], P('shard')
- mlp_gain_grad: float32 [1024], P('shard')
- gate_proj_grad: float32 [1024, 3072], P('shard')
- up_proj_grad: float32 [1024, 3072], P('shard')
- down_proj_grad: float32 [3072, 1024], P('shard')
The draws below stay inside these ranges and needn't reach their ends.
All inputs are finite; a program needn't handle non-finite values.
Results may differ from the reference program's by a relative error of at most 0.02.
Values may be sent and summed in bfloat16 or wider, within the bound.
A program may use at most 192 MiB of HBM per device.

```python
import jax
import jax.numpy as jnp
from jax import lax

D = 1024
H = 16
KV = 8
HD = 128
FF = 3072
TOK_DEV = 512
TOKENS = 16384


def with_spikes(array, key, source, target, parts, factor):
    owner, partner = [(jnp.arange(array.shape[axis_at]) // (array.shape[axis_at] // parts)).reshape([-1 if axis == axis_at else 1 for axis in range(array.ndim)]) for axis_at in (source, target)]
    chosen = jax.random.permutation(key, parts)[partner]
    strong = (owner == chosen) | (owner == (partner + parts // 2) % parts)
    return jnp.where(strong, factor * array, array)


def steps_of(stream_key, dims, shards, smallest, largest):
    def one(dim, blocks):
        steps = jax.random.uniform(jax.random.fold_in(jax.random.fold_in(stream_key, 6), dim), (blocks,), jnp.float32, smallest / len(shards), largest / len(shards))
        return jnp.repeat(jnp.exp(steps), dims[dim] // blocks).reshape((-1,) + (1,) * (len(dims) - dim - 1))

    level = one(*shards[0])
    for cut in shards[1:]:
        level = level * one(*cut)
    return level


def scatter_about(stream_key, shape, scale, most, pieces=(), kind=jnp.bfloat16):
    array = scale * jax.random.normal(stream_key, shape, jnp.float32)
    if pieces:
        array = array * steps_of(stream_key, shape, pieces, -0.22, 0.18)
    return jnp.clip(array, -most, most).astype(kind)


def noise_with(stream_key, shape, spread, most, shards, heavy, kind=jnp.bfloat16):
    values = spread * jax.random.normal(stream_key, shape, jnp.float32)
    if shards:
        values = values * steps_of(stream_key, shape, shards, -0.22, 0.18)
    return jnp.clip(with_spikes(values, jax.random.fold_in(stream_key, 3), *heavy), -most, most).astype(kind)


def setup_inputs(seed: int = 0) -> dict:
    key_list = jax.random.split(jax.random.key(seed), 14)
    tokens = noise_with(key_list[0], (TOKENS, D), 1.0, 6.0, ((0, 32),), (0, 1, 32, 2.75))
    cotangent = scatter_about(key_list[1], (TOKENS, D), 1.0, 6.0, ((0, 32),))
    attn_gain = jnp.clip(1.0 + 0.1 * jax.random.normal(key_list[2], (D,), jnp.float32), 0.5, 1.5).astype(jnp.bfloat16)
    query_gain = jnp.clip(1.0 + 0.15 * jax.random.normal(key_list[3], (HD,), jnp.float32), 0.25, 1.75).astype(jnp.bfloat16)
    key_gain = jnp.clip(1.0 + 0.15 * jax.random.normal(key_list[4], (HD,), jnp.float32), 0.25, 1.75).astype(jnp.bfloat16)
    query_proj = scatter_about(key_list[5], (D, H * HD), D ** -0.5, 0.1875, ((0, 8),))
    key_proj = scatter_about(key_list[6], (D, KV * HD), D ** -0.5, 0.1875, ((0, 8),))
    value_proj = scatter_about(key_list[7], (D, KV * HD), D ** -0.5, 0.1875, ((0, 8),))
    out_proj = scatter_about(key_list[8], (H * HD, D), 64 ** -0.5, 0.75, ((0, 8),))
    mlp_gain = jnp.clip(1.0 + 0.1 * jax.random.normal(key_list[9], (D,), jnp.float32), 0.5, 1.5).astype(jnp.bfloat16)
    gate_proj = scatter_about(key_list[10], (D, FF), D ** -0.5, 0.1875, ((0, 8),))
    up_proj = scatter_about(key_list[11], (D, FF), D ** -0.5, 0.1875, ((0, 8),))
    down_proj = scatter_about(key_list[12], (FF, D), FF ** -0.5, 0.109375, ((0, 8),))
    return dict(tokens=tokens, cotangent=cotangent, attn_gain=attn_gain, query_gain=query_gain, key_gain=key_gain, query_proj=query_proj, key_proj=key_proj, value_proj=value_proj, out_proj=out_proj, mlp_gain=mlp_gain, gate_proj=gate_proj, up_proj=up_proj, down_proj=down_proj)


EPS = 1e-06
THETA = 1000000.0
HIGHEST_PRECISION = lax.Precision.HIGHEST

@jax.custom_vjp
def low(v):
    return lax.optimization_barrier(v.astype(jnp.bfloat16)).astype(jnp.float32)

@jax.custom_vjp
def low_back(v):
    return v

def low_keep(v):
    return (low(v), None)

def low_pass(kept, grad):
    return (grad,)

def back_keep(v):
    return (v, None)

def back_low(kept, grad):
    return (low(grad),)
low.defvjp(low_keep, low_pass)
low_back.defvjp(back_keep, back_low)

def product(left, right):
    return jnp.dot(left, right, precision=HIGHEST_PRECISION, preferred_element_type=jnp.float32)

def rotary_tables(length, width):
    half_width = width // 2
    frequency = THETA ** (-(jnp.arange(half_width, dtype=jnp.float32) * 2.0) / width)
    angles = jnp.arange(length, dtype=jnp.float32)[:, None] * frequency[None, :]
    angles = jnp.concatenate([angles, angles], axis=1)
    return (jnp.cos(angles)[:, None, :], jnp.sin(angles)[:, None, :])

def rotate(values):
    half_width = values.shape[-1] // 2
    return jnp.concatenate([-values[..., half_width:], values[..., :half_width]], axis=-1)

def rms_apply(values, gain):
    return values * lax.rsqrt(lax.optimization_barrier(jnp.mean(values * values, axis=-1, keepdims=True)) + EPS) * gain

def block_forward(inputs, attn_gain, query_gain, key_gain, query_proj, key_proj, value_proj, out_proj, mlp_gain, gate_proj, up_proj, down_proj):
    length = inputs.shape[0]
    group_size = H // KV
    cosine, sine = rotary_tables(length, HD)
    normed = low(rms_apply(inputs, attn_gain))
    query_raw = low_back(product(normed, query_proj)).reshape(length, H, HD)
    key_raw = low_back(product(normed, key_proj)).reshape(length, KV, HD)
    value_b = low(low_back(product(normed, value_proj))).reshape(length, KV, HD)
    query_normed = rms_apply(query_raw, query_gain)
    key_normed = rms_apply(key_raw, key_gain)
    query_rot = low(query_normed * cosine + rotate(query_normed) * sine).reshape(length, KV, group_size, HD)
    key_rot = low(key_normed * cosine + rotate(key_normed) * sine)
    scores = jnp.einsum('qgjd,kgd->gjqk', query_rot, key_rot, precision=HIGHEST_PRECISION) * HD ** (-0.5)
    scores = low_back(scores)
    causal = jnp.arange(length)[:, None] >= jnp.arange(length)[None, :]
    scores = jnp.where(causal, scores, -1e+30)
    highest = lax.optimization_barrier(jnp.max(scores, axis=-1, keepdims=True))
    powers = jnp.exp(scores - highest)
    attention_probs = low(powers / lax.optimization_barrier(jnp.sum(powers, axis=-1, keepdims=True)))
    mixed = jnp.einsum('gjqk,kgd->qgjd', attention_probs, value_b, precision=HIGHEST_PRECISION).reshape(length, H * HD)
    mixed = low(low_back(mixed))
    middle = inputs + low_back(product(mixed, out_proj))
    inner = low(rms_apply(middle, mlp_gain))
    gate_value = low_back(product(inner, gate_proj))
    up_value = low_back(product(inner, up_proj))
    hidden = low(jax.nn.silu(gate_value) * up_value)
    return middle + low_back(product(hidden, down_proj))

def reference(tokens, cotangent, attn_gain, query_gain, key_gain, query_proj, key_proj, value_proj, out_proj, mlp_gain, gate_proj, up_proj, down_proj):
    weights = tuple((item.astype(jnp.float32) for item in (attn_gain, query_gain, key_gain, query_proj, key_proj, value_proj, out_proj, mlp_gain, gate_proj, up_proj, down_proj)))
    sequences = tokens.astype(jnp.float32).reshape(TOKENS // TOK_DEV, TOK_DEV, D)
    cotangents = cotangent.astype(jnp.float32).reshape(TOKENS // TOK_DEV, TOK_DEV, D)

    def sequence_step(totals, pair):
        inputs, grad_out = pair
        output, pullback = jax.vjp(block_forward, inputs, *weights)
        gradients = pullback(grad_out)
        totals = tuple((first + second for first, second in zip(totals, gradients[1:])))
        return (totals, (output, gradients[0]))
    initial = tuple((jnp.zeros(item.shape, jnp.float32) for item in weights))
    totals, (outputs, input_grads) = lax.scan(sequence_step, initial, (sequences, cotangents))
    return (outputs.reshape(TOKENS, D).astype(jnp.bfloat16), input_grads.reshape(TOKENS, D), totals[0], totals[1], totals[2], totals[3], totals[4], totals[5], totals[6], totals[7], totals[8], totals[9], totals[10])
```

```python
import jax
import jax.numpy as jnp
from jax import lax
from jax.sharding import PartitionSpec as P

EPS = 1e-06
THETA = 1000000.0


def product(left, right):
    return jnp.dot(left, right, preferred_element_type=jnp.float32)


def left_product(left, right):
    return lax.dot_general(
        left, right, (((0,), (0,)), ((), ())), preferred_element_type=jnp.float32
    )


def right_product(left, right):
    return lax.dot_general(
        left, right, (((1,), (1,)), ((), ())), preferred_element_type=jnp.float32
    )


def rotary_tables(length, width):
    half_width = width // 2
    frequency = THETA ** (-(jnp.arange(half_width, dtype=jnp.float32) * 2.0) / width)
    angles = jnp.arange(length, dtype=jnp.float32)[:, None] * frequency[None, :]
    angles = jnp.concatenate([angles, angles], axis=1)
    return (jnp.cos(angles)[:, None, :], jnp.sin(angles)[:, None, :])


def rotate(values):
    half_width = values.shape[-1] // 2
    return jnp.concatenate([-values[..., half_width:], values[..., :half_width]], axis=-1)


def rotate_back(values):
    half_width = values.shape[-1] // 2
    return jnp.concatenate([values[..., half_width:], -values[..., :half_width]], axis=-1)


def inverse_rms(values):
    return lax.rsqrt(jnp.mean(values * values, axis=-1, keepdims=True) + EPS)


def norm_back(grads, values, inverse, gain):
    weighted = grads * gain
    return inverse * weighted - values * (inverse * inverse * inverse) * jnp.mean(
        weighted * values, axis=-1, keepdims=True
    )


def masked_scores(query_b, key_b):
    head_size = query_b.shape[-1]
    length = query_b.shape[0]
    scores = jnp.einsum(
        "qgjd,kgd->gjqk", query_b, key_b, preferred_element_type=jnp.float32
    ) * head_size ** (-0.5)
    causal = jnp.arange(length)[:, None] >= jnp.arange(length)[None, :]
    return jnp.where(causal, scores, -1e30)


def attend(query_b, key_b, value_b):
    scores = masked_scores(query_b, key_b)
    highest = jnp.max(scores, axis=-1, keepdims=True)
    powers = jnp.exp(scores - highest)
    totals = jnp.sum(powers, axis=-1, keepdims=True)
    probs_b = (powers / totals).astype(jnp.bfloat16)
    mixed = jnp.einsum("gjqk,kgd->qgjd", probs_b, value_b, preferred_element_type=jnp.float32)
    return (mixed, highest + jnp.log(totals))


def attend_back(query_b, key_b, value_b, log_totals, grad_mixed):
    head_size = query_b.shape[-1]
    probs = jnp.exp(masked_scores(query_b, key_b) - log_totals)
    probs_b = probs.astype(jnp.bfloat16)
    grad_probs = jnp.einsum(
        "qgjd,kgd->gjqk", grad_mixed, value_b, preferred_element_type=jnp.float32
    )
    value_grad = jnp.einsum(
        "gjqk,qgjd->kgd", probs_b, grad_mixed, preferred_element_type=jnp.float32
    )
    grad_scores = probs * (grad_probs - jnp.sum(probs * grad_probs, axis=-1, keepdims=True))
    grad_scores = grad_scores.astype(jnp.bfloat16)
    grad_qrot = jnp.einsum(
        "gjqk,kgd->qgjd", grad_scores, key_b, preferred_element_type=jnp.float32
    ) * head_size ** (-0.5)
    grad_krot = jnp.einsum(
        "gjqk,qgjd->kgd", grad_scores, query_b, preferred_element_type=jnp.float32
    ) * head_size ** (-0.5)
    return (grad_qrot, grad_krot, value_grad)


def sibling_pairs(count):
    return [(i, i ^ 1) for i in range(count)]


def from_sibling(values):
    return lax.ppermute(values, "rep", sibling_pairs(lax.axis_size("rep")))


def half_columns(values, core):
    width = values.shape[1] // 2
    return lax.dynamic_slice_in_dim(values, core * width, width, axis=1)


def in_order(mine, other, core):
    first = core == 0
    return jnp.concatenate([jnp.where(first, mine, other), jnp.where(first, other, mine)], axis=-1)


def gather_pair(block):
    mine = lax.all_gather(block, "shard", axis=0, tiled=True)
    return (mine, from_sibling(mine))


def scatter_pair(mine, other):
    received = from_sibling(other.astype(jnp.bfloat16))
    pair = (mine + received.astype(jnp.float32)).astype(jnp.bfloat16)
    part = lax.psum_scatter(pair, "shard", scatter_dimension=0, tiled=True)
    count = lax.axis_size("rep")
    groups = [list(range(c, count, 2)) for c in range(2)]
    return lax.psum(part, "rep", axis_index_groups=groups)


def shards(
    tokens,
    cotangent,
    attn_gain,
    query_gain,
    key_gain,
    query_proj,
    key_proj,
    value_proj,
    out_proj,
    mlp_gain,
    gate_proj,
    up_proj,
    down_proj,
):
    core = lax.rem(lax.axis_index("rep"), 2)
    size = lax.axis_size("shard")
    width = tokens.shape[1]
    head_size = query_gain.shape[0] * size
    query_heads = query_proj.shape[1] // head_size
    key_heads = key_proj.shape[1] // head_size
    group_size = query_heads // key_heads
    length = tokens.shape[0]
    gains = lax.all_gather(
        jnp.concatenate([attn_gain, mlp_gain, query_gain, key_gain]), "shard", axis=0, tiled=False
    ).astype(jnp.float32)
    step = width // size
    small = head_size // size
    attn_scale = gains[:, :step].reshape(width)
    mlp_scale = gains[:, step : 2 * step].reshape(width)
    query_scale = gains[:, 2 * step : 2 * step + small].reshape(head_size)
    key_scale = gains[:, 2 * step + small :].reshape(head_size)
    qkv = gather_pair(
        jnp.concatenate([half_columns(w, core) for w in (query_proj, key_proj, value_proj)], axis=1)
    )
    outs = gather_pair(half_columns(out_proj, core))
    gate_up = gather_pair(
        jnp.concatenate([half_columns(w, core) for w in (gate_proj, up_proj)], axis=1)
    )
    downs = gather_pair(half_columns(down_proj, core))

    q_half = query_proj.shape[1] // 2
    k_half = key_proj.shape[1] // 2
    ff_half = gate_proj.shape[1] // 2
    inputs = tokens.astype(jnp.float32)
    cosine, sine = rotary_tables(length, head_size)
    inv_one = inverse_rms(inputs)
    normed = (inputs * inv_one * attn_scale).astype(jnp.bfloat16)
    raws = [product(normed, w) for w in qkv]
    query_raw = jnp.concatenate([r[:, :q_half] for r in raws], axis=1).reshape(
        length, query_heads, head_size
    )
    key_raw = jnp.concatenate([r[:, q_half : q_half + k_half] for r in raws], axis=1).reshape(
        length, key_heads, head_size
    )
    value_b = (
        jnp.concatenate([r[:, q_half + k_half :] for r in raws], axis=1)
        .astype(jnp.bfloat16)
        .reshape(length, key_heads, head_size)
    )
    inv_query = inverse_rms(query_raw)
    inv_key = inverse_rms(key_raw)
    query_normed = query_raw * inv_query * query_scale
    key_normed = key_raw * inv_key * key_scale
    query_rot = (
        (query_normed * cosine + rotate(query_normed) * sine)
        .astype(jnp.bfloat16)
        .reshape(length, key_heads, group_size, head_size)
    )
    key_rot = (key_normed * cosine + rotate(key_normed) * sine).astype(jnp.bfloat16)
    mixed, log_totals = attend(query_rot, key_rot, value_b)
    mixed_b = mixed.reshape(length, query_heads * head_size).astype(jnp.bfloat16)
    mixed_b = in_order(mixed_b[:, :q_half], mixed_b[:, q_half:], core)
    middle = inputs + in_order(product(mixed_b, outs[0]), product(mixed_b, outs[1]), core)
    inv_two = inverse_rms(middle)
    inner = (middle * inv_two * mlp_scale).astype(jnp.bfloat16)
    cot = [half_columns(cotangent, core), half_columns(cotangent, 1 - core)]
    gates_ups = [product(inner, w) for w in gate_up]
    gate_values = [v[:, :ff_half] for v in gates_ups]
    up_values = [v[:, ff_half:] for v in gates_ups]
    hiddens = [
        (jax.nn.silu(g) * u).astype(jnp.bfloat16) for g, u in zip(gate_values, up_values)
    ]
    hidden = in_order(hiddens[0], hiddens[1], core)
    layer_out = (
        middle + in_order(product(hidden, downs[0]), product(hidden, downs[1]), core)
    ).astype(jnp.bfloat16)
    grad_hidden = right_product(cot[0], downs[0]) + right_product(cot[1], downs[1])
    grad_hiddens = [half_columns(grad_hidden, core), half_columns(grad_hidden, 1 - core)]
    down_part = scatter_pair(left_product(hidden, cot[0]), left_product(hidden, cot[1]))
    grads = []
    for g, u, grad in zip(gate_values, up_values, grad_hiddens):
        sigmoid = jax.nn.sigmoid(g)
        grads.append(
            jnp.concatenate(
                [
                    (grad * u * (sigmoid + g * sigmoid * (1.0 - sigmoid))).astype(jnp.bfloat16),
                    (grad * (g * sigmoid)).astype(jnp.bfloat16),
                ],
                axis=1,
            )
        )
    gate_up_part = scatter_pair(left_product(inner, grads[0]), left_product(inner, grads[1]))
    grad_inner = right_product(grads[0], gate_up[0]) + right_product(grads[1], gate_up[1])
    mlp_gain_grad = jnp.sum(grad_inner * middle * inv_two, axis=0)
    grad_middle = cotangent.astype(jnp.float32) + norm_back(grad_inner, middle, inv_two, mlp_scale)
    grad_attn = grad_middle.astype(jnp.bfloat16)
    grad_attns = [half_columns(grad_attn, core), half_columns(grad_attn, 1 - core)]
    out_part = scatter_pair(
        left_product(mixed_b, grad_attns[0]), left_product(mixed_b, grad_attns[1])
    )
    grad_mixed = (
        right_product(grad_attns[0], outs[0]) + right_product(grad_attns[1], outs[1])
    ).astype(jnp.bfloat16)
    grad_mixed = jnp.concatenate(
        [half_columns(grad_mixed, core), half_columns(grad_mixed, 1 - core)], axis=1
    ).reshape(length, key_heads, group_size, head_size)
    grad_qrot, grad_krot, value_grad = attend_back(
        query_rot, key_rot, value_b, log_totals, grad_mixed
    )
    grad_qrot = grad_qrot.reshape(length, query_heads, head_size)
    grad_qnorm = grad_qrot * cosine + rotate_back(grad_qrot * sine)
    grad_knorm = grad_krot * cosine + rotate_back(grad_krot * sine)
    query_gain_grad = jnp.sum(grad_qnorm * query_raw * inv_query, axis=(0, 1))
    key_gain_grad = jnp.sum(grad_knorm * key_raw * inv_key, axis=(0, 1))
    grad_query = norm_back(grad_qnorm, query_raw, inv_query, query_scale)
    grad_query = grad_query.astype(jnp.bfloat16).reshape(length, query_heads * head_size)
    grad_key = norm_back(grad_knorm, key_raw, inv_key, key_scale)
    grad_key = grad_key.astype(jnp.bfloat16).reshape(length, key_heads * head_size)
    value_grad = value_grad.astype(jnp.bfloat16).reshape(length, key_heads * head_size)
    grad_qkv = [
        jnp.concatenate([grad_query[:, :q_half], grad_key[:, :k_half], value_grad[:, :k_half]], 1),
        jnp.concatenate([grad_query[:, q_half:], grad_key[:, k_half:], value_grad[:, k_half:]], 1),
    ]
    qkv_part = scatter_pair(left_product(normed, grad_qkv[0]), left_product(normed, grad_qkv[1]))
    grad_normed = right_product(grad_qkv[0], qkv[0]) + right_product(grad_qkv[1], qkv[1])
    attn_gain_grad = jnp.sum(grad_normed * inputs * inv_one, axis=0)
    tokens_grad = grad_middle + norm_back(grad_normed, inputs, inv_one, attn_scale)

    gain_grads = jnp.concatenate(
        [
            attn_gain_grad.reshape(size, step),
            mlp_gain_grad.reshape(size, step),
            query_gain_grad.reshape(size, small),
            key_gain_grad.reshape(size, small),
        ],
        axis=1,
    )
    gain_sums = lax.psum(gain_grads, ("rep", "shard"))
    gain_sums = lax.dynamic_index_in_dim(
        gain_sums, lax.axis_index("shard"), axis=0, keepdims=False
    )

    parts = [qkv_part, out_part, gate_up_part, down_part]
    others = [from_sibling(p) for p in parts]

    def whole(index, start, stop):
        return in_order(
            parts[index][:, start:stop].astype(jnp.float32),
            others[index][:, start:stop].astype(jnp.float32),
            core,
        )

    return (
        layer_out,
        tokens_grad,
        gain_sums[:step],
        gain_sums[2 * step : 2 * step + small],
        gain_sums[2 * step + small :],
        whole(0, 0, q_half),
        whole(0, q_half, q_half + k_half),
        whole(0, q_half + k_half, q_half + 2 * k_half),
        whole(1, 0, width // 2),
        gain_sums[step : 2 * step],
        whole(2, 0, ff_half),
        whole(2, ff_half, 2 * ff_half),
        whole(3, 0, width // 2),
    )


def solution(mesh):
    in_specs = (
        P(("rep", "shard"), None),
        P(("rep", "shard"), None),
        P("shard"),
        P("shard"),
        P("shard"),
        P("shard", None),
        P("shard", None),
        P("shard", None),
        P("shard", None),
        P("shard"),
        P("shard", None),
        P("shard", None),
        P("shard", None),
    )
    out_specs = (
        P(("rep", "shard"), None),
        P(("rep", "shard"), None),
        P("shard"),
        P("shard"),
        P("shard"),
        P("shard", None),
        P("shard", None),
        P("shard", None),
        P("shard", None),
        P("shard"),
        P("shard", None),
        P("shard", None),
        P("shard", None),
    )
    return jax.shard_map(shards, mesh=mesh, in_specs=in_specs, out_specs=out_specs, check_vma=False)
```

```python
import functools

import jax
import jax.numpy as jnp
from jax import lax
from jax.experimental import pallas as pl
from jax.experimental.pallas import tpu as pltpu
from jax.sharding import PartitionSpec as P

EPS = 1e-06
THETA = 1000000.0


def product(left, right):
    return jnp.dot(left, right, preferred_element_type=jnp.float32)


def left_product(left, right):
    return lax.dot_general(
        left, right, (((0,), (0,)), ((), ())), preferred_element_type=jnp.float32
    )


def right_product(left, right):
    return lax.dot_general(
        left, right, (((1,), (1,)), ((), ())), preferred_element_type=jnp.float32
    )


def rotary_tables(length, width):
    half_width = width // 2
    frequency = THETA ** (-(jnp.arange(half_width, dtype=jnp.float32) * 2.0) / width)
    angles = jnp.arange(length, dtype=jnp.float32)[:, None] * frequency[None, :]
    angles = jnp.concatenate([angles, angles], axis=1)
    return (jnp.cos(angles)[:, None, :], jnp.sin(angles)[:, None, :])


def rotate(values):
    half_width = values.shape[-1] // 2
    return jnp.concatenate([-values[..., half_width:], values[..., :half_width]], axis=-1)


def rotate_back(values):
    half_width = values.shape[-1] // 2
    return jnp.concatenate([values[..., half_width:], -values[..., :half_width]], axis=-1)


def inverse_rms(values):
    return lax.rsqrt(jnp.mean(values * values, axis=-1, keepdims=True) + EPS)


def norm_back(grads, values, inverse, gain):
    weighted = grads * gain
    return inverse * weighted - values * (inverse * inverse * inverse) * jnp.mean(
        weighted * values, axis=-1, keepdims=True
    )


def masked_scores(query_b, key_b):
    head_size = query_b.shape[-1]
    length = query_b.shape[0]
    scores = jnp.einsum(
        "qgjd,kgd->gjqk", query_b, key_b, preferred_element_type=jnp.float32
    ) * head_size ** (-0.5)
    causal = jnp.arange(length)[:, None] >= jnp.arange(length)[None, :]
    return jnp.where(causal, scores, -1e30)


def attend(query_b, key_b, value_b):
    scores = masked_scores(query_b, key_b)
    highest = jnp.max(scores, axis=-1, keepdims=True)
    powers = jnp.exp(scores - highest)
    totals = jnp.sum(powers, axis=-1, keepdims=True)
    probs_b = (powers / totals).astype(jnp.bfloat16)
    mixed = jnp.einsum("gjqk,kgd->qgjd", probs_b, value_b, preferred_element_type=jnp.float32)
    return (mixed, highest + jnp.log(totals))


def attend_back(query_b, key_b, value_b, log_totals, grad_mixed):
    head_size = query_b.shape[-1]
    probs = jnp.exp(masked_scores(query_b, key_b) - log_totals)
    probs_b = probs.astype(jnp.bfloat16)
    grad_probs = jnp.einsum(
        "qgjd,kgd->gjqk", grad_mixed, value_b, preferred_element_type=jnp.float32
    )
    value_grad = jnp.einsum(
        "gjqk,qgjd->kgd", probs_b, grad_mixed, preferred_element_type=jnp.float32
    )
    grad_scores = probs * (grad_probs - jnp.sum(probs * grad_probs, axis=-1, keepdims=True))
    grad_scores = grad_scores.astype(jnp.bfloat16)
    grad_qrot = jnp.einsum(
        "gjqk,kgd->qgjd", grad_scores, key_b, preferred_element_type=jnp.float32
    ) * head_size ** (-0.5)
    grad_krot = jnp.einsum(
        "gjqk,qgjd->kgd", grad_scores, query_b, preferred_element_type=jnp.float32
    ) * head_size ** (-0.5)
    return (grad_qrot, grad_krot, value_grad)


def sibling_pairs(count):
    return [(i, i ^ 1) for i in range(count)]


def from_sibling(values):
    return lax.ppermute(values, "rep", sibling_pairs(lax.axis_size("rep")))


def half_columns(values, core):
    width = values.shape[1] // 2
    return lax.dynamic_slice_in_dim(values, core * width, width, axis=1)


def in_order(mine, other, core):
    first = core == 0
    return jnp.concatenate([jnp.where(first, mine, other), jnp.where(first, other, mine)], axis=-1)


def gather_pair(block):
    mine = lax.all_gather(block, "shard", axis=0, tiled=True)
    return (mine, from_sibling(mine))


def scatter_pair(mine, other):
    received = from_sibling(other.astype(jnp.bfloat16))
    pair = (mine + received.astype(jnp.float32)).astype(jnp.bfloat16)
    part = lax.psum_scatter(pair, "shard", scatter_dimension=0, tiled=True)
    count = lax.axis_size("rep")
    groups = [list(range(c, count, 2)) for c in range(2)]
    return lax.psum(part, "rep", axis_index_groups=groups)


MESH = pl.DeviceIdType.MESH


def ring_member(place, size):
    place = lax.rem(place + 2 * size, size)
    back = place // (size // 2)
    return (1 - back) * (2 * place) + back * (2 * (size - 1 - place) + 1)


def ring_place(size):
    index = lax.axis_index("shard")
    odd = lax.rem(index, 2)
    row = index // 2
    return (1 - odd) * row + odd * (size - 1 - row)


def sibling():
    rep = lax.axis_index("rep")
    return {"rep": rep + 1 - 2 * lax.rem(rep, 2)}


def greet(devices):
    barrier = pltpu.get_barrier_semaphore()
    for device in devices:
        pl.semaphore_signal(barrier, inc=1, device_id=device, device_id_type=MESH)
    pl.semaphore_wait(barrier, len(devices))


def rows_of(ref, index, way):
    rows = ref.shape[1] // 2
    return ref.at[index, pl.ds(way * rows, rows)]


def gather_kernel(size, count, *refs):
    blocks, mine, other = refs[:count], refs[count : 2 * count], refs[2 * count : 3 * count]
    ring_send, ring_recv, pair_send, pair_recv, local = refs[3 * count :]
    me = lax.axis_index("shard")
    place = ring_place(size)
    pair = sibling()
    near = [{"shard": ring_member(place + 1, size)}, {"shard": ring_member(place - 1, size)}]
    greet(near + [pair])

    def send(src, dst, sems, step, way, i, device):
        copy = pltpu.make_async_remote_copy(
            src_ref=src,
            dst_ref=dst,
            send_sem=sems[0].at[step, way, i],
            recv_sem=sems[1].at[step, way, i],
            device_id=device,
            device_id_type=MESH,
        )
        copy.start()
        return copy

    ring_sems, pair_sems = (ring_send, ring_recv), (pair_send, pair_recv)
    ring, pairs, locals_ = {}, [], []
    for step in range(size):
        for i in range(count):
            for way in range(2):
                index = ring_member(place - step if way == 0 else place + step, size)
                rows = blocks[i].shape[0] // 2
                if step == 0:
                    src = blocks[i].at[pl.ds(way * rows, rows)]
                else:
                    ring[step - 1, way, i].wait_recv()
                    src = rows_of(mine[i], index, way)
                if step < size - 1:
                    ring[step, way, i] = send(
                        src, rows_of(mine[i], index, way), ring_sems, step, way, i, near[way]
                    )
                pairs.append(
                    send(src, rows_of(other[i], index, way), pair_sems, step, way, i, pair)
                )
        if step == 0:
            for i in range(count):
                copy = pltpu.make_async_copy(blocks[i], mine[i].at[me], local.at[i])
                copy.start()
                locals_.append(copy)
    for copy in locals_:
        copy.wait()
    for copy in ring.values():
        copy.wait_send()
    for copy in pairs:
        copy.wait()


def ring_gather(blocks, size):
    count = len(blocks)
    shapes = [jax.ShapeDtypeStruct((size,) + b.shape, b.dtype) for b in blocks]
    sems = pltpu.SemaphoreType.DMA((size, 2, count))
    total = sum(b.size * 2 for b in blocks) * size
    results = pl.pallas_call(
        functools.partial(gather_kernel, size, count),
        out_shape=shapes + shapes,
        in_specs=[pl.BlockSpec(memory_space=pl.ANY)] * count,
        out_specs=[pl.BlockSpec(memory_space=pl.ANY)] * (2 * count),
        scratch_shapes=[sems, sems, sems, sems, pltpu.SemaphoreType.DMA((count,))],
        compiler_params=pltpu.CompilerParams(collective_id=0, has_side_effects=True),
        cost_estimate=pl.CostEstimate(flops=0, bytes_accessed=30 * total, transcendentals=0),
    )(*blocks)
    results = [r.reshape(-1, r.shape[-1]) for r in results]
    return list(zip(results[:count], results[count:]))


def scatter_kernel(size, groups, count, *refs):
    mine, other = refs[:count], refs[count : 2 * count]
    out, out_pair = refs[2 * count : 3 * count], refs[3 * count : 4 * count]
    held, arrived = refs[4 * count : 5 * count], refs[5 * count : 6 * count]
    sums = refs[6 * count : 7 * count]
    pair_send, pair_recv, ring_send, ring_recv, rep_send, rep_recv, end_send, end_recv = refs[
        7 * count :
    ]
    place = ring_place(size)
    rep = lax.axis_index("rep")
    core = lax.rem(rep, 2)
    group = rep // 2
    pair = sibling()
    near = [{"shard": ring_member(place + 1, size)}, {"shard": ring_member(place - 1, size)}]
    peers = [{"rep": 2 * lax.rem(group + d, groups) + core} for d in range(1, groups)]
    greet(near + [pair] + peers)

    def send(src, dst, send_sem, recv_sem, device):
        copy = pltpu.make_async_remote_copy(
            src_ref=src,
            dst_ref=dst,
            send_sem=send_sem,
            recv_sem=recv_sem,
            device_id=device,
            device_id_type=MESH,
        )
        copy.start()
        return copy

    def owner(step, way):
        return ring_member(place - 1 - step if way == 0 else place + 1 + step, size)

    pairs, ring = {}, {}
    for step in range(size):
        for i in range(count):
            for way in range(2):
                index = owner(step, way)
                at = (step, way, i)
                pairs[at] = send(
                    rows_of(other[i], index, way),
                    rows_of(held[i], index, way),
                    pair_send.at[at],
                    pair_recv.at[at],
                    pair,
                )
    for step in range(size):
        for i in range(count):
            rows = mine[i].shape[1] // 2
            for way in range(2):
                index = owner(step, way)
                here = pl.ds(way * rows, rows)
                at = (step, way, i)
                pairs[at].wait_recv()
                total = mine[i][index, here].astype(jnp.float32) + held[i][index, here].astype(
                    jnp.float32
                )
                if step > 0:
                    ring[step - 1, way, i].wait_recv()
                    total = total + arrived[i][step - 1, here].astype(jnp.float32)
                total = total.astype(jnp.bfloat16)
                if step < size - 1:
                    held[i][index, here] = total
                    ring[at] = send(
                        rows_of(held[i], index, way),
                        rows_of(arrived[i], step, way),
                        ring_send.at[at],
                        ring_recv.at[at],
                        near[way],
                    )
                else:
                    sums[i][group, here] = total
    reps = []
    for i in range(count):
        for d in range(1, groups):
            reps.append(
                send(
                    sums[i].at[group],
                    sums[i].at[group],
                    rep_send.at[d, i],
                    rep_recv.at[d, i],
                    peers[d - 1],
                )
            )
    for copy in reps:
        copy.wait()
    ends = []
    for i in range(count):
        total = sums[i][0].astype(jnp.float32)
        for g in range(1, groups):
            total = total + sums[i][g].astype(jnp.float32)
        out[i][...] = total.astype(jnp.bfloat16)
        ends.append(send(out[i], out_pair[i], end_send.at[i], end_recv.at[i], pair))
    for copy in ends:
        copy.wait()
    for copy in ring.values():
        copy.wait_send()
    for copy in pairs.values():
        copy.wait_send()


def ring_scatter(mine, other, size, groups):
    count = len(mine)
    mine = [m.astype(jnp.bfloat16).reshape(size, -1, m.shape[-1]) for m in mine]
    other = [m.astype(jnp.bfloat16).reshape(size, -1, m.shape[-1]) for m in other]
    shapes = [jax.ShapeDtypeStruct(m.shape[1:], m.dtype) for m in mine]
    vmem = pl.BlockSpec(memory_space=pltpu.VMEM)
    sems = pltpu.SemaphoreType.DMA((size, 2, count))
    rep_sems = pltpu.SemaphoreType.DMA((groups, count))
    end_sems = pltpu.SemaphoreType.DMA((count,))
    total = sum(m.size * 2 for m in mine)
    results = pl.pallas_call(
        functools.partial(scatter_kernel, size, groups, count),
        out_shape=shapes + shapes,
        in_specs=[vmem] * (2 * count),
        out_specs=[vmem] * (2 * count),
        scratch_shapes=[pltpu.VMEM(m.shape, m.dtype) for m in mine]
        + [pltpu.VMEM((size - 1,) + m.shape[1:], m.dtype) for m in mine]
        + [pltpu.VMEM((groups,) + m.shape[1:], m.dtype) for m in mine]
        + [sems, sems, sems, sems, rep_sems, rep_sems, end_sems, end_sems],
        compiler_params=pltpu.CompilerParams(
            collective_id=1, has_side_effects=True, vmem_limit_bytes=48 * 1024 * 1024
        ),
        cost_estimate=pl.CostEstimate(flops=0, bytes_accessed=30 * total, transcendentals=0),
    )(*mine, *other)
    return list(zip(results[:count], results[count:]))


def shards(
    tokens,
    cotangent,
    attn_gain,
    query_gain,
    key_gain,
    query_proj,
    key_proj,
    value_proj,
    out_proj,
    mlp_gain,
    gate_proj,
    up_proj,
    down_proj,
):
    core = lax.rem(lax.axis_index("rep"), 2)
    size = lax.axis_size("shard")
    width = tokens.shape[1]
    head_size = query_gain.shape[0] * size
    query_heads = query_proj.shape[1] // head_size
    key_heads = key_proj.shape[1] // head_size
    group_size = query_heads // key_heads
    length = tokens.shape[0]
    step = width // size
    small = head_size // size
    lanes = -(-2 * (step + small) // 128) * 128
    gain_block = jnp.pad(
        jnp.concatenate([attn_gain, mlp_gain, query_gain, key_gain]),
        (0, lanes - 2 * (step + small)),
    )
    gain_pair, qkv, outs = ring_gather(
        [
            jnp.broadcast_to(gain_block[None], (32, lanes)),
            jnp.concatenate(
                [half_columns(w, core) for w in (query_proj, key_proj, value_proj)], axis=1
            ),
            half_columns(out_proj, core),
        ],
        size,
    )
    gains = gain_pair[0].reshape(size, 32, lanes)[:, 0].astype(jnp.float32)
    attn_scale = gains[:, :step].reshape(width)
    mlp_scale = gains[:, step : 2 * step].reshape(width)
    query_scale = gains[:, 2 * step : 2 * step + small].reshape(head_size)
    key_scale = gains[:, 2 * step + small : 2 * (step + small)].reshape(head_size)
    gate_up = gather_pair(
        jnp.concatenate([half_columns(w, core) for w in (gate_proj, up_proj)], axis=1)
    )
    downs = gather_pair(half_columns(down_proj, core))

    q_half = query_proj.shape[1] // 2
    k_half = key_proj.shape[1] // 2
    ff_half = gate_proj.shape[1] // 2
    inputs = tokens.astype(jnp.float32)
    cosine, sine = rotary_tables(length, head_size)
    inv_one = inverse_rms(inputs)
    normed = (inputs * inv_one * attn_scale).astype(jnp.bfloat16)
    raws = [product(normed, w) for w in qkv]
    query_raw = jnp.concatenate([r[:, :q_half] for r in raws], axis=1).reshape(
        length, query_heads, head_size
    )
    key_raw = jnp.concatenate([r[:, q_half : q_half + k_half] for r in raws], axis=1).reshape(
        length, key_heads, head_size
    )
    value_b = (
        jnp.concatenate([r[:, q_half + k_half :] for r in raws], axis=1)
        .astype(jnp.bfloat16)
        .reshape(length, key_heads, head_size)
    )
    inv_query = inverse_rms(query_raw)
    inv_key = inverse_rms(key_raw)
    query_normed = query_raw * inv_query * query_scale
    key_normed = key_raw * inv_key * key_scale
    query_rot = (
        (query_normed * cosine + rotate(query_normed) * sine)
        .astype(jnp.bfloat16)
        .reshape(length, key_heads, group_size, head_size)
    )
    key_rot = (key_normed * cosine + rotate(key_normed) * sine).astype(jnp.bfloat16)
    mixed, log_totals = attend(query_rot, key_rot, value_b)
    mixed_b = mixed.reshape(length, query_heads * head_size).astype(jnp.bfloat16)
    mixed_b = in_order(mixed_b[:, :q_half], mixed_b[:, q_half:], core)
    middle = inputs + in_order(product(mixed_b, outs[0]), product(mixed_b, outs[1]), core)
    inv_two = inverse_rms(middle)
    inner = (middle * inv_two * mlp_scale).astype(jnp.bfloat16)
    cot = [half_columns(cotangent, core), half_columns(cotangent, 1 - core)]
    gates_ups = [product(inner, w) for w in gate_up]
    gate_values = [v[:, :ff_half] for v in gates_ups]
    up_values = [v[:, ff_half:] for v in gates_ups]
    hiddens = [
        (jax.nn.silu(g) * u).astype(jnp.bfloat16) for g, u in zip(gate_values, up_values)
    ]
    hidden = in_order(hiddens[0], hiddens[1], core)
    layer_out = (
        middle + in_order(product(hidden, downs[0]), product(hidden, downs[1]), core)
    ).astype(jnp.bfloat16)
    grad_hidden = right_product(cot[0], downs[0]) + right_product(cot[1], downs[1])
    grad_hiddens = [half_columns(grad_hidden, core), half_columns(grad_hidden, 1 - core)]
    down_part = scatter_pair(left_product(hidden, cot[0]), left_product(hidden, cot[1]))
    grads = []
    for g, u, grad in zip(gate_values, up_values, grad_hiddens):
        sigmoid = jax.nn.sigmoid(g)
        grads.append(
            jnp.concatenate(
                [
                    (grad * u * (sigmoid + g * sigmoid * (1.0 - sigmoid))).astype(jnp.bfloat16),
                    (grad * (g * sigmoid)).astype(jnp.bfloat16),
                ],
                axis=1,
            )
        )
    gate_up_part = scatter_pair(left_product(inner, grads[0]), left_product(inner, grads[1]))
    grad_inner = right_product(grads[0], gate_up[0]) + right_product(grads[1], gate_up[1])
    mlp_gain_grad = jnp.sum(grad_inner * middle * inv_two, axis=0)
    grad_middle = cotangent.astype(jnp.float32) + norm_back(grad_inner, middle, inv_two, mlp_scale)
    grad_attn = grad_middle.astype(jnp.bfloat16)
    grad_attns = [half_columns(grad_attn, core), half_columns(grad_attn, 1 - core)]
    out_grads = [left_product(mixed_b, g) for g in grad_attns]
    grad_mixed = (
        right_product(grad_attns[0], outs[0]) + right_product(grad_attns[1], outs[1])
    ).astype(jnp.bfloat16)
    grad_mixed = jnp.concatenate(
        [half_columns(grad_mixed, core), half_columns(grad_mixed, 1 - core)], axis=1
    ).reshape(length, key_heads, group_size, head_size)
    grad_qrot, grad_krot, value_grad = attend_back(
        query_rot, key_rot, value_b, log_totals, grad_mixed
    )
    grad_qrot = grad_qrot.reshape(length, query_heads, head_size)
    grad_qnorm = grad_qrot * cosine + rotate_back(grad_qrot * sine)
    grad_knorm = grad_krot * cosine + rotate_back(grad_krot * sine)
    query_gain_grad = jnp.sum(grad_qnorm * query_raw * inv_query, axis=(0, 1))
    key_gain_grad = jnp.sum(grad_knorm * key_raw * inv_key, axis=(0, 1))
    grad_query = norm_back(grad_qnorm, query_raw, inv_query, query_scale)
    grad_query = grad_query.astype(jnp.bfloat16).reshape(length, query_heads * head_size)
    grad_key = norm_back(grad_knorm, key_raw, inv_key, key_scale)
    grad_key = grad_key.astype(jnp.bfloat16).reshape(length, key_heads * head_size)
    value_grad = value_grad.astype(jnp.bfloat16).reshape(length, key_heads * head_size)
    grad_qkv = [
        jnp.concatenate([grad_query[:, :q_half], grad_key[:, :k_half], value_grad[:, :k_half]], 1),
        jnp.concatenate([grad_query[:, q_half:], grad_key[:, k_half:], value_grad[:, k_half:]], 1),
    ]
    qkv_grads = [left_product(normed, g) for g in grad_qkv]
    grad_normed = right_product(grad_qkv[0], qkv[0]) + right_product(grad_qkv[1], qkv[1])
    attn_gain_grad = jnp.sum(grad_normed * inputs * inv_one, axis=0)
    tokens_grad = grad_middle + norm_back(grad_normed, inputs, inv_one, attn_scale)

    gain_grads = jnp.concatenate(
        [
            attn_gain_grad.reshape(size, step),
            mlp_gain_grad.reshape(size, step),
            query_gain_grad.reshape(size, small),
            key_gain_grad.reshape(size, small),
        ],
        axis=1,
    )
    gain_grads = jnp.pad(gain_grads, ((0, 0), (0, lanes - gain_grads.shape[1])))
    gain_grads = jnp.broadcast_to(gain_grads[:, None], (size, 32, lanes))
    gain_pair, qkv_pair, out_pair = ring_scatter(
        [gain_grads, qkv_grads[0], out_grads[0]],
        [gain_grads, qkv_grads[1], out_grads[1]],
        size,
        lax.axis_size("rep") // 2,
    )
    gain_sums = gain_pair[0][0].astype(jnp.float32)
    parts = [qkv_pair[0], out_pair[0], gate_up_part, down_part]
    others = [qkv_pair[1], out_pair[1], from_sibling(gate_up_part), from_sibling(down_part)]

    def whole(index, start, stop):
        return in_order(
            parts[index][:, start:stop].astype(jnp.float32),
            others[index][:, start:stop].astype(jnp.float32),
            core,
        )

    return (
        layer_out,
        tokens_grad,
        gain_sums[:step],
        gain_sums[2 * step : 2 * step + small],
        gain_sums[2 * step + small : 2 * (step + small)],
        whole(0, 0, q_half),
        whole(0, q_half, q_half + k_half),
        whole(0, q_half + k_half, q_half + 2 * k_half),
        whole(1, 0, width // 2),
        gain_sums[step : 2 * step],
        whole(2, 0, ff_half),
        whole(2, ff_half, 2 * ff_half),
        whole(3, 0, width // 2),
    )


def solution(mesh):
    in_specs = (
        P(("rep", "shard"), None),
        P(("rep", "shard"), None),
        P("shard"),
        P("shard"),
        P("shard"),
        P("shard", None),
        P("shard", None),
        P("shard", None),
        P("shard", None),
        P("shard"),
        P("shard", None),
        P("shard", None),
        P("shard", None),
    )
    out_specs = (
        P(("rep", "shard"), None),
        P(("rep", "shard"), None),
        P("shard"),
        P("shard"),
        P("shard"),
        P("shard", None),
        P("shard", None),
        P("shard", None),
        P("shard", None),
        P("shard"),
        P("shard", None),
        P("shard", None),
        P("shard", None),
    )
    return jax.shard_map(shards, mesh=mesh, in_specs=in_specs, out_specs=out_specs, check_vma=False)
```

```python
import functools

import jax
import jax.numpy as jnp
from jax import lax
from jax.experimental import pallas as pl
from jax.experimental.pallas import tpu as pltpu
from jax.sharding import PartitionSpec as P

EPS = 1e-06
THETA = 1000000.0


def product(left, right):
    return jnp.dot(left, right, preferred_element_type=jnp.float32)


def left_product(left, right):
    return lax.dot_general(
        left, right, (((0,), (0,)), ((), ())), preferred_element_type=jnp.float32
    )


def right_product(left, right):
    return lax.dot_general(
        left, right, (((1,), (1,)), ((), ())), preferred_element_type=jnp.float32
    )


def rotary_tables(length, width):
    half_width = width // 2
    frequency = THETA ** (-(jnp.arange(half_width, dtype=jnp.float32) * 2.0) / width)
    angles = jnp.arange(length, dtype=jnp.float32)[:, None] * frequency[None, :]
    angles = jnp.concatenate([angles, angles], axis=1)
    return (jnp.cos(angles)[:, None, :], jnp.sin(angles)[:, None, :])


def rotate(values):
    half_width = values.shape[-1] // 2
    return jnp.concatenate([-values[..., half_width:], values[..., :half_width]], axis=-1)


def rotate_back(values):
    half_width = values.shape[-1] // 2
    return jnp.concatenate([values[..., half_width:], -values[..., :half_width]], axis=-1)


def inverse_rms(values):
    return lax.rsqrt(jnp.mean(values * values, axis=-1, keepdims=True) + EPS)


def norm_back(grads, values, inverse, gain):
    weighted = grads * gain
    return inverse * weighted - values * (inverse * inverse * inverse) * jnp.mean(
        weighted * values, axis=-1, keepdims=True
    )


def masked_scores(query_b, key_b):
    head_size = query_b.shape[-1]
    length = query_b.shape[0]
    scores = jnp.einsum(
        "qgjd,kgd->gjqk", query_b, key_b, preferred_element_type=jnp.float32
    ) * head_size ** (-0.5)
    causal = jnp.arange(length)[:, None] >= jnp.arange(length)[None, :]
    return jnp.where(causal, scores, -1e30)


def attend(query_b, key_b, value_b):
    scores = masked_scores(query_b, key_b)
    highest = jnp.max(scores, axis=-1, keepdims=True)
    powers = jnp.exp(scores - highest)
    totals = jnp.sum(powers, axis=-1, keepdims=True)
    probs_b = (powers / totals).astype(jnp.bfloat16)
    mixed = jnp.einsum("gjqk,kgd->qgjd", probs_b, value_b, preferred_element_type=jnp.float32)
    return (mixed, highest + jnp.log(totals))


def attend_back(query_b, key_b, value_b, log_totals, grad_mixed):
    head_size = query_b.shape[-1]
    probs = jnp.exp(masked_scores(query_b, key_b) - log_totals)
    probs_b = probs.astype(jnp.bfloat16)
    grad_probs = jnp.einsum(
        "qgjd,kgd->gjqk", grad_mixed, value_b, preferred_element_type=jnp.float32
    )
    value_grad = jnp.einsum(
        "gjqk,qgjd->kgd", probs_b, grad_mixed, preferred_element_type=jnp.float32
    )
    grad_scores = probs * (grad_probs - jnp.sum(probs * grad_probs, axis=-1, keepdims=True))
    grad_scores = grad_scores.astype(jnp.bfloat16)
    grad_qrot = jnp.einsum(
        "gjqk,kgd->qgjd", grad_scores, key_b, preferred_element_type=jnp.float32
    ) * head_size ** (-0.5)
    grad_krot = jnp.einsum(
        "gjqk,qgjd->kgd", grad_scores, query_b, preferred_element_type=jnp.float32
    ) * head_size ** (-0.5)
    return (grad_qrot, grad_krot, value_grad)


def sibling_pairs(count):
    return [(i, i ^ 1) for i in range(count)]


def from_sibling(values):
    return lax.ppermute(values, "rep", sibling_pairs(lax.axis_size("rep")))


def half_columns(values, core):
    width = values.shape[1] // 2
    return lax.dynamic_slice_in_dim(values, core * width, width, axis=1)


def in_order(mine, other, core):
    first = core == 0
    return jnp.concatenate([jnp.where(first, mine, other), jnp.where(first, other, mine)], axis=-1)


def gather_pair(block):
    mine = lax.all_gather(block, "shard", axis=0, tiled=True)
    return (mine, from_sibling(mine))


def scatter_pair(mine, other):
    received = from_sibling(other.astype(jnp.bfloat16))
    pair = (mine + received.astype(jnp.float32)).astype(jnp.bfloat16)
    return lax.psum_scatter(pair, "shard", scatter_dimension=0, tiled=True)


MESH = pl.DeviceIdType.MESH


def ring_member(place, size):
    place = lax.rem(place + 2 * size, size)
    back = place // (size // 2)
    return (1 - back) * (2 * place) + back * (2 * (size - 1 - place) + 1)


def ring_place(size):
    index = lax.axis_index("shard")
    odd = lax.rem(index, 2)
    row = index // 2
    return (1 - odd) * row + odd * (size - 1 - row)


def sibling():
    rep = lax.axis_index("rep")
    return {"rep": rep + 1 - 2 * lax.rem(rep, 2)}


def greet(devices):
    barrier = pltpu.get_barrier_semaphore()
    for device in devices:
        pl.semaphore_signal(barrier, inc=1, device_id=device, device_id_type=MESH)
    pl.semaphore_wait(barrier, len(devices))


def rows_of(ref, index, way):
    rows = ref.shape[1] // 2
    return ref.at[index, pl.ds(way * rows, rows)]


def gather_kernel(size, count, *refs):
    blocks, mine, other = refs[:count], refs[count : 2 * count], refs[2 * count : 3 * count]
    ring_send, ring_recv, pair_send, pair_recv, local = refs[3 * count :]
    me = lax.axis_index("shard")
    place = ring_place(size)
    pair = sibling()
    near = [{"shard": ring_member(place + 1, size)}, {"shard": ring_member(place - 1, size)}]
    greet(near + [pair])

    def send(src, dst, sems, step, way, i, device):
        copy = pltpu.make_async_remote_copy(
            src_ref=src,
            dst_ref=dst,
            send_sem=sems[0].at[step, way, i],
            recv_sem=sems[1].at[step, way, i],
            device_id=device,
            device_id_type=MESH,
        )
        copy.start()
        return copy

    ring_sems, pair_sems = (ring_send, ring_recv), (pair_send, pair_recv)
    ring, pairs, locals_ = {}, [], []
    for step in range(size):
        for i in range(count):
            for way in range(2):
                index = ring_member(place - step if way == 0 else place + step, size)
                rows = blocks[i].shape[0] // 2
                if step == 0:
                    src = blocks[i].at[pl.ds(way * rows, rows)]
                else:
                    ring[step - 1, way, i].wait_recv()
                    src = rows_of(mine[i], index, way)
                if step < size - 1:
                    ring[step, way, i] = send(
                        src, rows_of(mine[i], index, way), ring_sems, step, way, i, near[way]
                    )
                pairs.append(
                    send(src, rows_of(other[i], index, way), pair_sems, step, way, i, pair)
                )
        if step == 0:
            for i in range(count):
                copy = pltpu.make_async_copy(blocks[i], mine[i].at[me], local.at[i])
                copy.start()
                locals_.append(copy)
    for copy in locals_:
        copy.wait()
    for copy in ring.values():
        copy.wait_send()
    for copy in pairs:
        copy.wait()


def ring_gather(blocks, size):
    count = len(blocks)
    shapes = [jax.ShapeDtypeStruct((size,) + b.shape, b.dtype) for b in blocks]
    sems = pltpu.SemaphoreType.DMA((size, 2, count))
    total = sum(b.size * 2 for b in blocks) * size
    results = pl.pallas_call(
        functools.partial(gather_kernel, size, count),
        out_shape=shapes + shapes,
        in_specs=[pl.BlockSpec(memory_space=pl.ANY)] * count,
        out_specs=[pl.BlockSpec(memory_space=pl.ANY)] * (2 * count),
        scratch_shapes=[sems, sems, sems, sems, pltpu.SemaphoreType.DMA((count,))],
        compiler_params=pltpu.CompilerParams(collective_id=0, has_side_effects=True),
        cost_estimate=pl.CostEstimate(flops=0, bytes_accessed=30 * total, transcendentals=0),
    )(*blocks)
    results = [r.reshape(-1, r.shape[-1]) for r in results]
    return list(zip(results[:count], results[count:]))


def scatter_kernel(size, groups, count, extra, *refs):
    refs = list(refs)

    def take(number):
        taken = refs[:number]
        del refs[:number]
        return taken

    every = count + extra
    mine, other, parts = take(count), take(count), take(extra)
    out, out_pair = take(every), take(every)
    held, arrived, sums = take(count), take(count), take(every)
    pair_send, pair_recv, ring_send, ring_recv, rep_send, rep_recv, end_send, end_recv = refs
    place = ring_place(size)
    rep = lax.axis_index("rep")
    core = lax.rem(rep, 2)
    group = rep // 2
    pair = sibling()
    near = [{"shard": ring_member(place + 1, size)}, {"shard": ring_member(place - 1, size)}]
    peers = [{"rep": 2 * lax.rem(group + d, groups) + core} for d in range(1, groups)]
    greet(near + [pair] + peers)

    def send(src, dst, send_sem, recv_sem, device):
        copy = pltpu.make_async_remote_copy(
            src_ref=src,
            dst_ref=dst,
            send_sem=send_sem,
            recv_sem=recv_sem,
            device_id=device,
            device_id_type=MESH,
        )
        copy.start()
        return copy

    def owner(step, way):
        return ring_member(place - 1 - step if way == 0 else place + 1 + step, size)

    pairs, ring = {}, {}
    for step in range(size):
        for i in range(count):
            for way in range(2):
                index = owner(step, way)
                at = (step, way, i)
                pairs[at] = send(
                    rows_of(other[i], index, way),
                    rows_of(held[i], index, way),
                    pair_send.at[at],
                    pair_recv.at[at],
                    pair,
                )
    reps = []

    def exchange(i):
        for d in range(1, groups):
            reps.append(
                send(
                    sums[i].at[group],
                    sums[i].at[group],
                    rep_send.at[d, i],
                    rep_recv.at[d, i],
                    peers[d - 1],
                )
            )

    for i in range(extra):
        sums[count + i][group] = parts[i][...]
        exchange(count + i)
    for step in range(size):
        for i in range(count):
            rows = mine[i].shape[1] // 2
            for way in range(2):
                index = owner(step, way)
                here = pl.ds(way * rows, rows)
                at = (step, way, i)
                pairs[at].wait_recv()
                total = mine[i][index, here].astype(jnp.float32) + held[i][index, here].astype(
                    jnp.float32
                )
                if step > 0:
                    ring[step - 1, way, i].wait_recv()
                    total = total + arrived[i][step - 1, here].astype(jnp.float32)
                total = total.astype(jnp.bfloat16)
                if step < size - 1:
                    held[i][index, here] = total
                    ring[at] = send(
                        rows_of(held[i], index, way),
                        rows_of(arrived[i], step, way),
                        ring_send.at[at],
                        ring_recv.at[at],
                        near[way],
                    )
                else:
                    sums[i][group, here] = total
    for i in range(count):
        exchange(i)
    for copy in reps:
        copy.wait()
    ends = []
    for i in range(every):
        total = sums[i][0].astype(jnp.float32)
        for g in range(1, groups):
            total = total + sums[i][g].astype(jnp.float32)
        out[i][...] = total.astype(jnp.bfloat16)
        ends.append(send(out[i], out_pair[i], end_send.at[i], end_recv.at[i], pair))
    for copy in ends:
        copy.wait()
    for copy in ring.values():
        copy.wait_send()
    for copy in pairs.values():
        copy.wait_send()


def ring_scatter(mine, other, parts, size, groups):
    count, extra = len(mine), len(parts)
    every = count + extra
    mine = [m.astype(jnp.bfloat16).reshape(size, -1, m.shape[-1]) for m in mine]
    other = [m.astype(jnp.bfloat16).reshape(size, -1, m.shape[-1]) for m in other]
    shapes = [jax.ShapeDtypeStruct(m.shape[1:], m.dtype) for m in mine]
    shapes += [jax.ShapeDtypeStruct(p.shape, p.dtype) for p in parts]
    vmem = pl.BlockSpec(memory_space=pltpu.VMEM)
    sems = pltpu.SemaphoreType.DMA((size, 2, count))
    rep_sems = pltpu.SemaphoreType.DMA((groups, every))
    end_sems = pltpu.SemaphoreType.DMA((every,))
    total = sum(m.size * 2 for m in mine)
    results = pl.pallas_call(
        functools.partial(scatter_kernel, size, groups, count, extra),
        out_shape=shapes + shapes,
        in_specs=[vmem] * (2 * count + extra),
        out_specs=[vmem] * (2 * every),
        scratch_shapes=[pltpu.VMEM(m.shape, m.dtype) for m in mine]
        + [pltpu.VMEM((size - 1,) + m.shape[1:], m.dtype) for m in mine]
        + [pltpu.VMEM((groups,) + shape.shape, shape.dtype) for shape in shapes]
        + [sems, sems, sems, sems, rep_sems, rep_sems, end_sems, end_sems],
        compiler_params=pltpu.CompilerParams(
            collective_id=1, has_side_effects=True, vmem_limit_bytes=48 * 1024 * 1024
        ),
        cost_estimate=pl.CostEstimate(flops=0, bytes_accessed=30 * total, transcendentals=0),
    )(*mine, *other, *parts)
    return list(zip(results[:every], results[every:]))


def shards(
    tokens,
    cotangent,
    attn_gain,
    query_gain,
    key_gain,
    query_proj,
    key_proj,
    value_proj,
    out_proj,
    mlp_gain,
    gate_proj,
    up_proj,
    down_proj,
):
    core = lax.rem(lax.axis_index("rep"), 2)
    size = lax.axis_size("shard")
    width = tokens.shape[1]
    head_size = query_gain.shape[0] * size
    query_heads = query_proj.shape[1] // head_size
    key_heads = key_proj.shape[1] // head_size
    group_size = query_heads // key_heads
    length = tokens.shape[0]
    step = width // size
    small = head_size // size
    lanes = -(-2 * (step + small) // 128) * 128
    gain_block = jnp.pad(
        jnp.concatenate([attn_gain, mlp_gain, query_gain, key_gain]),
        (0, lanes - 2 * (step + small)),
    )
    gain_pair, qkv, outs = ring_gather(
        [
            jnp.broadcast_to(gain_block[None], (32, lanes)),
            jnp.concatenate(
                [half_columns(w, core) for w in (query_proj, key_proj, value_proj)], axis=1
            ),
            half_columns(out_proj, core),
        ],
        size,
    )
    gains = gain_pair[0].reshape(size, 32, lanes)[:, 0].astype(jnp.float32)
    attn_scale = gains[:, :step].reshape(width)
    mlp_scale = gains[:, step : 2 * step].reshape(width)
    query_scale = gains[:, 2 * step : 2 * step + small].reshape(head_size)
    key_scale = gains[:, 2 * step + small : 2 * (step + small)].reshape(head_size)
    gate_up_block = jnp.concatenate([half_columns(w, core) for w in (gate_proj, up_proj)], axis=1)
    gate_up_block, down_block, gains = lax.optimization_barrier(
        (gate_up_block, half_columns(down_proj, core), gains)
    )
    gate_up = gather_pair(gate_up_block)
    downs = gather_pair(down_block)

    q_half = query_proj.shape[1] // 2
    k_half = key_proj.shape[1] // 2
    ff_half = gate_proj.shape[1] // 2
    inputs = tokens.astype(jnp.float32)
    cosine, sine = rotary_tables(length, head_size)
    inv_one = inverse_rms(inputs)
    normed = (inputs * inv_one * attn_scale).astype(jnp.bfloat16)
    raws = [product(normed, w) for w in qkv]
    query_raw = jnp.concatenate([r[:, :q_half] for r in raws], axis=1).reshape(
        length, query_heads, head_size
    )
    key_raw = jnp.concatenate([r[:, q_half : q_half + k_half] for r in raws], axis=1).reshape(
        length, key_heads, head_size
    )
    value_b = (
        jnp.concatenate([r[:, q_half + k_half :] for r in raws], axis=1)
        .astype(jnp.bfloat16)
        .reshape(length, key_heads, head_size)
    )
    inv_query = inverse_rms(query_raw)
    inv_key = inverse_rms(key_raw)
    query_normed = query_raw * inv_query * query_scale
    key_normed = key_raw * inv_key * key_scale
    query_rot = (
        (query_normed * cosine + rotate(query_normed) * sine)
        .astype(jnp.bfloat16)
        .reshape(length, key_heads, group_size, head_size)
    )
    key_rot = (key_normed * cosine + rotate(key_normed) * sine).astype(jnp.bfloat16)
    mixed, log_totals = attend(query_rot, key_rot, value_b)
    mixed_b = mixed.reshape(length, query_heads * head_size).astype(jnp.bfloat16)
    mixed_b = in_order(mixed_b[:, :q_half], mixed_b[:, q_half:], core)
    middle = inputs + in_order(product(mixed_b, outs[0]), product(mixed_b, outs[1]), core)
    inv_two = inverse_rms(middle)
    inner = (middle * inv_two * mlp_scale).astype(jnp.bfloat16)
    cot = [half_columns(cotangent, core), half_columns(cotangent, 1 - core)]
    gates_ups = [product(inner, w) for w in gate_up]
    gate_values = [v[:, :ff_half] for v in gates_ups]
    up_values = [v[:, ff_half:] for v in gates_ups]
    hiddens = [
        (jax.nn.silu(g) * u).astype(jnp.bfloat16) for g, u in zip(gate_values, up_values)
    ]
    hidden = in_order(hiddens[0], hiddens[1], core)
    layer_out = (
        middle + in_order(product(hidden, downs[0]), product(hidden, downs[1]), core)
    ).astype(jnp.bfloat16)
    grad_hidden = right_product(cot[0], downs[0]) + right_product(cot[1], downs[1])
    grad_hiddens = [half_columns(grad_hidden, core), half_columns(grad_hidden, 1 - core)]
    down_part = scatter_pair(left_product(hidden, cot[0]), left_product(hidden, cot[1]))
    grads = []
    for g, u, grad in zip(gate_values, up_values, grad_hiddens):
        sigmoid = jax.nn.sigmoid(g)
        grads.append(
            jnp.concatenate(
                [
                    (grad * u * (sigmoid + g * sigmoid * (1.0 - sigmoid))).astype(jnp.bfloat16),
                    (grad * (g * sigmoid)).astype(jnp.bfloat16),
                ],
                axis=1,
            )
        )
    gate_up_part = scatter_pair(left_product(inner, grads[0]), left_product(inner, grads[1]))
    grad_inner = right_product(grads[0], gate_up[0]) + right_product(grads[1], gate_up[1])
    mlp_gain_grad = jnp.sum(grad_inner * middle * inv_two, axis=0)
    grad_middle = cotangent.astype(jnp.float32) + norm_back(grad_inner, middle, inv_two, mlp_scale)
    grad_attn = grad_middle.astype(jnp.bfloat16)
    grad_attns = [half_columns(grad_attn, core), half_columns(grad_attn, 1 - core)]
    out_grads = [left_product(mixed_b, g) for g in grad_attns]
    grad_mixed = (
        right_product(grad_attns[0], outs[0]) + right_product(grad_attns[1], outs[1])
    ).astype(jnp.bfloat16)
    grad_mixed = jnp.concatenate(
        [half_columns(grad_mixed, core), half_columns(grad_mixed, 1 - core)], axis=1
    ).reshape(length, key_heads, group_size, head_size)
    grad_qrot, grad_krot, value_grad = attend_back(
        query_rot, key_rot, value_b, log_totals, grad_mixed
    )
    grad_qrot = grad_qrot.reshape(length, query_heads, head_size)
    grad_qnorm = grad_qrot * cosine + rotate_back(grad_qrot * sine)
    grad_knorm = grad_krot * cosine + rotate_back(grad_krot * sine)
    query_gain_grad = jnp.sum(grad_qnorm * query_raw * inv_query, axis=(0, 1))
    key_gain_grad = jnp.sum(grad_knorm * key_raw * inv_key, axis=(0, 1))
    grad_query = norm_back(grad_qnorm, query_raw, inv_query, query_scale)
    grad_query = grad_query.astype(jnp.bfloat16).reshape(length, query_heads * head_size)
    grad_key = norm_back(grad_knorm, key_raw, inv_key, key_scale)
    grad_key = grad_key.astype(jnp.bfloat16).reshape(length, key_heads * head_size)
    value_grad = value_grad.astype(jnp.bfloat16).reshape(length, key_heads * head_size)
    grad_qkv = [
        jnp.concatenate([grad_query[:, :q_half], grad_key[:, :k_half], value_grad[:, :k_half]], 1),
        jnp.concatenate([grad_query[:, q_half:], grad_key[:, k_half:], value_grad[:, k_half:]], 1),
    ]
    qkv_grads = [left_product(normed, g) for g in grad_qkv]
    grad_normed = right_product(grad_qkv[0], qkv[0]) + right_product(grad_qkv[1], qkv[1])
    attn_gain_grad = jnp.sum(grad_normed * inputs * inv_one, axis=0)
    tokens_grad = grad_middle + norm_back(grad_normed, inputs, inv_one, attn_scale)

    gain_grads = jnp.concatenate(
        [
            attn_gain_grad.reshape(size, step),
            mlp_gain_grad.reshape(size, step),
            query_gain_grad.reshape(size, small),
            key_gain_grad.reshape(size, small),
        ],
        axis=1,
    )
    gain_grads = jnp.pad(gain_grads, ((0, 0), (0, lanes - gain_grads.shape[1])))
    gain_grads = jnp.broadcast_to(gain_grads[:, None], (size, 32, lanes))
    gain_pair, qkv_pair, out_pair, gate_up_pair, down_pair = ring_scatter(
        [gain_grads, qkv_grads[0], out_grads[0]],
        [gain_grads, qkv_grads[1], out_grads[1]],
        [gate_up_part, down_part],
        size,
        lax.axis_size("rep") // 2,
    )
    gain_sums = gain_pair[0][0].astype(jnp.float32)
    pairs = [qkv_pair, out_pair, gate_up_pair, down_pair]
    parts, others = zip(*pairs)

    def whole(index, start, stop):
        return in_order(
            parts[index][:, start:stop].astype(jnp.float32),
            others[index][:, start:stop].astype(jnp.float32),
            core,
        )

    return (
        layer_out,
        tokens_grad,
        gain_sums[:step],
        gain_sums[2 * step : 2 * step + small],
        gain_sums[2 * step + small : 2 * (step + small)],
        whole(0, 0, q_half),
        whole(0, q_half, q_half + k_half),
        whole(0, q_half + k_half, q_half + 2 * k_half),
        whole(1, 0, width // 2),
        gain_sums[step : 2 * step],
        whole(2, 0, ff_half),
        whole(2, ff_half, 2 * ff_half),
        whole(3, 0, width // 2),
    )


def solution(mesh):
    in_specs = (
        P(("rep", "shard"), None),
        P(("rep", "shard"), None),
        P("shard"),
        P("shard"),
        P("shard"),
        P("shard", None),
        P("shard", None),
        P("shard", None),
        P("shard", None),
        P("shard"),
        P("shard", None),
        P("shard", None),
        P("shard", None),
    )
    out_specs = (
        P(("rep", "shard"), None),
        P(("rep", "shard"), None),
        P("shard"),
        P("shard"),
        P("shard"),
        P("shard", None),
        P("shard", None),
        P("shard", None),
        P("shard", None),
        P("shard"),
        P("shard", None),
        P("shard", None),
        P("shard", None),
    )
    return jax.shard_map(shards, mesh=mesh, in_specs=in_specs, out_specs=out_specs, check_vma=False)
```
